512 devices in a mesh: tm: 32 (over z, core), dp: 8 (over x_lo, y), rep: 2 (over x_hi).
Axes of the slice: x: 4 (x_hi: 2, x_lo: 2; x = x_hi * 2 + x_lo), y: 4, z: 16, core: 2. Of those that a mesh axis runs over, the one named last changes fastest.
Arguments:
- clip_frames: bfloat16 [16, 128, 32, 4, 256], P(('dp', 'rep'), 'tm'), may hold values from -6 to 6
- conv_weight: bfloat16 [3, 3, 3, 256, 256], replicated, may hold values from -0.078125 to 0.078125
- up_weight: bfloat16 [256, 1024], replicated, may hold values from -0.375 to 0.375
- cotangent: bfloat16 [16, 128, 32, 4, 1024], P(('dp', 'rep'), None, 'tm'), may hold values from -6 to 6
Outputs:
- input_grad: bfloat16 [16, 128, 32, 4, 256], P(('dp', 'rep'), 'tm')
- up_grad: float32 [256, 1024], P('tm', ('dp', 'rep'))
The draws below stay inside these ranges and needn't reach their ends.
All inputs are finite; a program needn't handle non-finite values.
Results may differ from the reference program's by a relative error of at most 0.012.
Values may be sent and summed in bfloat16 or wider, within the bound.
A program may use at most 128 MiB of HBM per device.

```python
import math
import jax
import jax.numpy as jnp
from jax import lax

C = 256
COLS = 4
CUP = 1024
T_SIZE = 128
H = 32
CLIPS = 16


def spiked(values, own_key, source, target, parts, factor):
    owner, partner = [(jnp.arange(values.shape[dim]) // (values.shape[dim] // parts)).reshape([-1 if axis == dim else 1 for axis in range(values.ndim)]) for dim in (source, target)]
    chosen = jax.random.permutation(own_key, parts)[partner]
    strong = (owner == chosen) | (owner == (partner + parts // 2) % parts)
    return jnp.where(strong, factor * values, values)


def shard_levels(rng, dims, cuts, low, largest):
    def one(dim, shards_of):
        steps = jax.random.uniform(jax.random.fold_in(jax.random.fold_in(rng, 6), dim), (shards_of,), jnp.float32, low / len(cuts), largest / len(cuts))
        return jnp.repeat(jnp.exp(steps), dims[dim] // shards_of).reshape((-1,) + (1,) * (len(dims) - dim - 1))

    loudness = one(*cuts[0])
    for cut in cuts[1:]:
        loudness = loudness * one(*cut)
    return loudness


def noise(own_key, dims, deviation, most, split=(), dtype=jnp.bfloat16):
    gain = shard_levels(own_key, dims, split, -0.22, 0.18) if split else 1.0
    drawn = jax.random.normal(own_key, dims, jnp.float32) * deviation * gain
    return jnp.minimum(jnp.maximum(drawn, -most), most).astype(dtype)


def gaussian_with(key, extent, scale, most, shards, heavy, dtype=jnp.bfloat16):
    array = scale * jax.random.normal(key, extent, jnp.float32)
    if shards:
        array = array * shard_levels(key, extent, shards, -0.22, 0.18)
    return jnp.clip(spiked(array, jax.random.fold_in(key, 3), *heavy), -most, most).astype(dtype)


def setup_inputs(seed: int = 0) -> dict:
    key_list = jax.random.split(jax.random.key(seed), 5)
    return {
        "clip_frames": noise(key_list[0], (CLIPS, T_SIZE, H, COLS, C), 1.0, 6.0, ((0, 16), (1, 32))),
        "conv_weight": noise(key_list[1], (3, 3, 3, C, C), (27 * C) ** -0.5, 0.078125),
        "up_weight": noise(key_list[2], (C, CUP), C ** -0.5, 0.375),
        "cotangent": gaussian_with(key_list[3], (CLIPS, T_SIZE, H, COLS, CUP), 1.0, 6.0, ((0, 16), (2, 32)), (0, 4, 16, 2.0)),
    }


def forward_pre(frames, kernel):
    padded = jnp.concatenate([frames[:1], frames[:1], frames], axis=0)
    result = lax.conv_general_dilated(padded[None], kernel, (1, 1, 1), [(0, 0), (1, 1), (1, 1)], dimension_numbers=('NDHWC', 'DHWIO', 'NDHWC'), precision=lax.Precision.HIGHEST)
    return result[0]

def reference(clip_frames, conv_weight, up_weight, cotangent):
    kernel = conv_weight.astype(jnp.float32)

    def one_clip(total, pair):
        frames, upstream = pair
        pre, pull = jax.vjp(lambda value: forward_pre(value, kernel), frames.astype(jnp.float32))
        flat_pre = pre.reshape(-1, C)
        hidden = jax.nn.silu(flat_pre).astype(jnp.bfloat16)
        flat_g = upstream.reshape(-1, upstream.shape[-1])
        term = lax.dot_general(hidden, flat_g, (((0,), (0,)), ((), ())), preferred_element_type=jnp.float32)
        hidden_grad = lax.dot_general(flat_g, up_weight, (((1,), (1,)), ((), ())), preferred_element_type=jnp.float32).astype(jnp.bfloat16)
        sigma = jax.nn.sigmoid(flat_pre)
        slope = sigma * (1.0 + flat_pre * (1.0 - sigma))
        pre_grad = (hidden_grad.astype(jnp.float32) * slope).astype(jnp.bfloat16)
        frame_grad, = pull(pre_grad.astype(jnp.float32).reshape(pre.shape))
        return (total + term, frame_grad.astype(jnp.bfloat16))
    total, input_grad = lax.scan(one_clip, jnp.zeros((C, 4 * C), jnp.float32), (clip_frames, cotangent))
    factor = 1.0 / math.sqrt(CLIPS * T_SIZE * H * COLS)
    return (input_grad, total * factor)
```

```python
import functools
import math

import jax
import jax.numpy as jnp
from jax import lax
from jax.experimental import pallas as pl
from jax.experimental.pallas import tpu as pltpu
from jax.sharding import PartitionSpec as P

MESH = pl.DeviceIdType.MESH
BF16 = jnp.bfloat16
F32 = jnp.float32
LANES = (slice(0, 128), slice(128, 256))


def dot_nn(a, b):
    return lax.dot_general(a, b, (((1,), (0,)), ((), ())), preferred_element_type=F32)


def dot_nt(a, b):
    return lax.dot_general(a, b, (((1,), (1,)), ((), ())), preferred_element_type=F32)


def kernel(n, J, R, factor, x_ref, w_hbm, u_ref, g_ref, out_ref, ug_ref,
           w, wt, gt, rg, hg, hid, hidr, hf, ph, phr, x32, p32, q32, s, pre, slope, of32,
           r1s, r1r, keep, r2s, r2r, r3s, r3r,
           w_sem, hf_sem, ph_sem, hg_sem, hid_sem, r1_sem, r2_sem, r3_send, r3_recv):
    H = n
    C = 256
    FW = 16
    HALF = 2 * 4 * H
    XP = 4 * H + 16
    QP = H + 16
    CB = 1024 // J
    RB = C // n
    me = lax.axis_index("tm")
    dp = lax.axis_index("dp")
    rep = lax.axis_index("rep")
    core = lax.rem(me, 2)
    myj = dp * R + rep
    is_first = me == 0
    is_last = me == n - 1

    def offset(k):
        return lax.rem(jnp.where(lax.rem(k, 2) == 1, (k + 1) // 2, n - k // 2), n)

    def peer(k):
        return lax.rem(me + offset(k), n)

    def block(i):
        return pl.ds(pl.multiple_of(i * FW, FW), FW)

    def to_tm(src, dst, sems, target):
        return pltpu.make_async_remote_copy(
            src_ref=src, dst_ref=dst, send_sem=sems.at[0], recv_sem=sems.at[1],
            device_id=(target, dp, rep), device_id_type=MESH)

    def to_xy(src, dst, sems, j):
        return pltpu.make_async_remote_copy(
            src_ref=src, dst_ref=dst, send_sem=sems.at[0], recv_sem=sems.at[1],
            device_id=(me, j // R, lax.rem(j, R)), device_id_type=MESH)

    barrier = pltpu.get_barrier_semaphore()
    wcopy = pltpu.make_async_copy(w_hbm, w, w_sem)
    wcopy.start()

    def greet_tm(k, _):
        pl.semaphore_signal(barrier, inc=1, device_id=(lax.rem(me + k, n), dp, rep), device_id_type=MESH)
        return 0

    def greet_xy(k, _):
        j = lax.rem(myj + k, J)
        pl.semaphore_signal(barrier, inc=1, device_id=(me, j // R, lax.rem(j, R)), device_id_type=MESH)
        return 0

    lax.fori_loop(1, n, greet_tm, 0)
    lax.fori_loop(1, J, greet_xy, 0)

    rg[...] = dot_nt(g_ref[...], u_ref[...]).astype(BF16)
    hg[block(me), :] = rg[block(me), :]

    pl.semaphore_wait(barrier, n - 1 + J - 1)

    halo = to_tm(x_ref.at[pl.ds(HALF, HALF)], hf, hf_sem, lax.rem(me + 1, n))

    @pl.when(jnp.logical_not(is_last))
    def _():
        halo.start()

    def send_hg(k, _):
        to = peer(k)
        to_tm(rg.at[block(to)], hg.at[block(me)], hg_sem, to).start()
        return 0

    lax.fori_loop(1, n, send_hg, 0)

    for f in range(6):
        x32[:, pl.ds(f * XP, 8), :] = jnp.zeros((2, 8, 128), F32)
        x32[:, pl.ds(f * XP + 8 + 4 * H, 8), :] = jnp.zeros((2, 8, 128), F32)
    for f in range(6):
        s[f, 0:H, :] = jnp.zeros((H, 3 * C), BF16)
        s[f, 5 * H : 6 * H, :] = jnp.zeros((H, 3 * C), BF16)

    def put_frame(f, ref, source):
        for e in range(2):
            x32[e, pl.ds(f * XP + 8, 4 * H), :] = ref[pl.ds(source * 4 * H, 4 * H), LANES[e]].astype(F32)

    for f in range(2, 6):
        put_frame(f, x_ref, f - 2)

    def shifts(f, _):
        for col in range(4):
            for b in range(3):
                for e in range(2):
                    v = x32[e, pl.ds(f * XP + 8 + (b - 1) * 4 + col, H, stride=4), :]
                    s[f, (col + 1) * H : (col + 2) * H, b * C + e * 128 : b * C + (e + 1) * 128] = v.astype(BF16)
        return 0

    lax.fori_loop(2, 6, shifts, 0)
    wcopy.wait()

    def set_pre(value):
        for e in range(2):
            pre[e] = value[:, LANES[e]]

    def add_pre(value):
        for e in range(2):
            pre[e] += value[:, LANES[e]]

    def conv_step(a, c):
        lhs = s[pl.ds(a, 4), pl.ds(pl.multiple_of(c * H, H), 4 * H), :].reshape(16 * H, 3 * C)
        return dot_nn(lhs, w[a, :, c].reshape(3 * C, C))

    set_pre(conv_step(2, 0))

    def conv_fwd(k, _):
        add_pre(conv_step(2 - k // 3, lax.rem(k, 3)))
        return 0

    lax.fori_loop(1, 3, conv_fwd, 0)

    @pl.when(jnp.logical_not(is_last))
    def _():
        halo.wait_send()

    @pl.when(jnp.logical_not(is_first))
    def _():
        halo.wait_recv()
        for f in range(2):
            put_frame(f, hf, f)

    @pl.when(is_first)
    def _():
        for f in range(2):
            put_frame(f, x_ref, 0)

    lax.fori_loop(0, 2, shifts, 0)
    lax.fori_loop(3, 9, conv_fwd, 0)

    def act(group, _):
        for u in range(4):
            k = group * 4 + u
            to = peer(k)
            for e in range(2):
                v = pre[e, pl.ds(to, FW, stride=H), :]
                sig = 1.0 / (1.0 + jnp.exp(-v))
                hid[block(to), LANES[e]] = (v * sig).astype(BF16)
                slope[block(to), LANES[e]] = sig * (1.0 + v * (1.0 - sig))
        for u in range(4):
            k = group * 4 + u
            to = peer(k)

            @pl.when(k > 0)
            def _():
                to_tm(hid.at[block(to)], hidr.at[block(me)], hid_sem, to).start()
        return 0

    lax.fori_loop(0, n // 4, act, 0)
    hidr[block(me), :] = hid[block(me), :]

    def flip_g(i, _):
        at = pl.multiple_of(i * 128, 128)
        gt[pl.ds(at, 128), :] = g_ref[:, pl.ds(at, 128)].T
        return 0

    lax.fori_loop(0, 8, flip_g, 0)

    def flip_w(k, _):
        a, c = k // 3, lax.rem(k, 3)
        for b in range(3):
            wt[k, b * C : (b + 1) * C, :] = w[2 - a, 2 - b, 2 - c].T
        return 0

    lax.fori_loop(0, 9, flip_w, 0)

    def all_blocks(src, dst, sems):
        most = pl.ds(0, (n - 1) * FW)
        return to_tm(src.at[most], dst.at[most], sems, lax.rem(me + 1, n))

    done_hid = all_blocks(hid, hidr, hid_sem)
    done_hid.wait_recv()
    theirs = pl.ds(pl.multiple_of((1 - core) * 128, 128), 128)
    mine = pl.ds(pl.multiple_of(core * 128, 128), 128)
    r1s[...] = dot_nn(gt[...], hidr[:, theirs]).astype(BF16)
    pair = to_tm(r1s, r1r, r1_sem, me + 1 - 2 * core)
    pair.start()
    keep[...] = dot_nn(gt[...], hidr[:, mine])
    pair.wait()
    keep[...] += r1r[...].astype(F32)
    r2s[...] = keep[...].astype(BF16)

    def rows_of(j):
        return pl.ds(pl.multiple_of(j * CB, CB), CB)

    def send_r2(k, _):
        j = lax.rem(myj + k, J)
        to_xy(r2s.at[rows_of(j)], r2r.at[rows_of(myj)], r2_sem, j).start()
        return 0

    lax.fori_loop(1, J, send_r2, 0)

    p32[:, pl.ds(0, FW), :] = jnp.zeros((2, FW, 128), F32)
    p32[:, pl.ds((H + 1) * FW, FW), :] = jnp.zeros((2, FW, 128), F32)
    done_hg = all_blocks(rg, hg, hg_sem)
    done_hg.wait_recv()
    grad = (hg[...].astype(F32) * slope[...]).astype(BF16)
    for e in range(2):
        p32[e, pl.ds(FW, H * FW), :] = grad[:, LANES[e]].astype(F32)

    def grad_shifts(t, _):
        for col in range(4):
            for b in range(3):
                for e in range(2):
                    v = p32[e, pl.ds(b * FW + t * 4 + col, H, stride=FW), :].astype(BF16)
                    s[t, (col + 1) * H : (col + 2) * H, b * C + e * 128 : b * C + (e + 1) * 128] = v
        return 0

    lax.fori_loop(0, 2, grad_shifts, 0)
    for t in range(2):
        ph[pl.ds(t * 4 * H, 4 * H), :] = s[t, H : 5 * H, C : 2 * C]
    back = to_tm(ph, phr, ph_sem, lax.rem(me + n - 1, n))

    @pl.when(jnp.logical_not(is_first))
    def _():
        back.start()

    lax.fori_loop(2, 4, grad_shifts, 0)

    @pl.when(is_first)
    def _():
        two = s[0].astype(F32) + s[1].astype(F32)
        s[6] = two.astype(BF16)
        s[7] = (two + s[2].astype(F32)).astype(BF16)

    def back_step(k):
        a, c = k // 3, lax.rem(k, 3)
        at = pl.ds(pl.multiple_of(c * H, H), 4 * H)
        head = jnp.where(jnp.logical_and(is_first, a > 0), a + 5, a)
        lhs = jnp.concatenate([s[pl.ds(head, 1), at, :], s[pl.ds(a + 1, 3), at, :]], axis=0)
        return dot_nn(lhs.reshape(16 * H, 3 * C), wt[k])

    set_pre(back_step(0))

    def conv_back(k, _):
        add_pre(back_step(k))
        return 0

    lax.fori_loop(1, 3, conv_back, 0)

    most_xy = pl.ds(0, (J - 1) * CB)
    done_r2 = to_xy(r2s.at[most_xy], r2r.at[most_xy], r2_sem, lax.rem(myj + 1, J))
    done_r2.wait_recv()
    r2r[rows_of(myj), :] = jnp.zeros((CB, 128), BF16)
    total = keep[rows_of(myj), :]
    for j in range(J):
        total = total + r2r[pl.ds(j * CB, CB), :].astype(F32)
    flipped = total.T
    for m in range(n // 2):
        r3s[m] = flipped[m * RB : (m + 1) * RB, :]

    z = me // 2

    def r3_copy(m):
        return pltpu.make_async_remote_copy(
            src_ref=r3s.at[m], dst_ref=r3r.at[z], send_sem=r3_send.at[m], recv_sem=r3_recv.at[z],
            device_id=(core * (n // 2) + m, dp, rep), device_id_type=MESH)

    def send_r3(m, _):
        @pl.when(core * (n // 2) + m != me)
        def _():
            r3_copy(m).start()

        @pl.when(core * (n // 2) + m == me)
        def _():
            r3r[z] = r3s[m]
        return 0

    lax.fori_loop(0, n // 2, send_r3, 0)

    for tw in range(8):
        q32[pl.ds(tw * QP, 8), :] = jnp.zeros((8, C), F32)
        q32[pl.ds(tw * QP + 8 + H, 8), :] = jnp.zeros((8, C), F32)

    @pl.when(jnp.logical_not(is_first))
    def _():
        back.wait_send()

    @pl.when(jnp.logical_not(is_last))
    def _():
        back.wait_recv()
        for tw in range(8):
            q32[pl.ds(tw * QP + 8, H), :] = phr[pl.ds(tw * H, H), :].astype(F32)

    @pl.when(is_last)
    def _():
        for tw in range(8):
            q32[pl.ds(tw * QP + 8, H), :] = jnp.zeros((H, C), F32)

    for t in range(2):
        for col in range(4):
            for b in range(3):
                v = q32[pl.ds((t * 4 + col) * QP + 7 + b, H), :].astype(BF16)
                s[4 + t, (col + 1) * H : (col + 2) * H, b * C : (b + 1) * C] = v

    lax.fori_loop(3, 9, conv_back, 0)

    for t in range(4):
        for col in range(4):
            for e in range(2):
                of32[e, pl.ds(t * 4 * H + col, H, stride=4), :] = pre[e, pl.ds((t * 4 + col) * H, H), :]
    for e in range(2):
        out_ref[:, LANES[e]] = of32[e].astype(BF16)

    def wait_r3(i, _):
        @pl.when(2 * i + me // (n // 2) != me)
        def _():
            pltpu.make_async_remote_copy(
                src_ref=r3s.at[i], dst_ref=r3r.at[i], send_sem=r3_send.at[i], recv_sem=r3_recv.at[i],
                device_id=(lax.rem(me + 1, n), dp, rep), device_id_type=MESH).wait_recv()

        @pl.when(core * (n // 2) + i != me)
        def _():
            r3_copy(i).wait_send()
        return 0

    lax.fori_loop(0, n // 2, wait_r3, 0)
    result = r3r[0]
    for i in range(1, n // 2):
        result = result + r3r[i]
    ug_ref[...] = result * factor

    done_hid.wait_send()
    done_hg.wait_send()
    done_r2.wait_send()


def local(n, J, R, clip_frames, conv_weight, up_weight, cotangent):
    C = conv_weight.shape[-1]
    H = n
    pixels = 16 * H
    factor = 1.0 / math.sqrt(J * 4 * n * H * 4)
    x = clip_frames.reshape(pixels, C)
    g = cotangent.reshape(16 * n, 4 * C)
    vmem = pl.BlockSpec(memory_space=pltpu.VMEM)
    pair = pltpu.SemaphoreType.DMA((2,))
    out, up = pl.pallas_call(
        functools.partial(kernel, n, J, R, factor),
        out_shape=(
            jax.ShapeDtypeStruct((pixels, C), BF16),
            jax.ShapeDtypeStruct((C // n, 4 * C // J), F32),
        ),
        in_specs=[vmem, pl.BlockSpec(memory_space=pl.ANY), vmem, vmem],
        out_specs=(vmem, vmem),
        scratch_shapes=[
            pltpu.VMEM((3, 3, 3, C, C), BF16),
            pltpu.VMEM((9, 3 * C, C), BF16),
            pltpu.VMEM((4 * C, 16 * n), BF16),
            pltpu.VMEM((16 * n, C), BF16),
            pltpu.VMEM((16 * n, C), BF16),
            pltpu.VMEM((16 * n, C), BF16),
            pltpu.VMEM((16 * n, C), BF16),
            pltpu.VMEM((8 * H, C), BF16),
            pltpu.VMEM((8 * H, C), BF16),
            pltpu.VMEM((8 * H, C), BF16),
            pltpu.VMEM((2, 6 * (4 * H + 16), 128), F32),
            pltpu.VMEM((2, (H + 2) * 16, 128), F32),
            pltpu.VMEM((8 * (H + 16), C), F32),
            pltpu.VMEM((8, 6 * H, 3 * C), BF16),
            pltpu.VMEM((2, pixels, 128), F32),
            pltpu.VMEM((pixels, C), F32),
            pltpu.VMEM((2, pixels, 128), F32),
            pltpu.VMEM((4 * C, C // 2), BF16),
            pltpu.VMEM((4 * C, C // 2), BF16),
            pltpu.VMEM((4 * C, C // 2), F32),
            pltpu.VMEM((4 * C, C // 2), BF16),
            pltpu.VMEM((4 * C, C // 2), BF16),
            pltpu.VMEM((n // 2, C // n, 4 * C // J), F32),
            pltpu.VMEM((n // 2, C // n, 4 * C // J), F32),
            pltpu.SemaphoreType.DMA,
            pair, pair, pair, pair, pair, pair,
            pltpu.SemaphoreType.DMA((n // 2,)),
            pltpu.SemaphoreType.DMA((n // 2,)),
        ],
        compiler_params=pltpu.CompilerParams(
            collective_id=0, has_side_effects=True, vmem_limit_bytes=48 * 1024 * 1024),
        cost_estimate=pl.CostEstimate(flops=4_200_000_000, bytes_accessed=6_000_000, transcendentals=131072),
    )(x, conv_weight, up_weight, g)
    return out.reshape(clip_frames.shape), up


def solution(mesh):
    in_specs = (
        P(("dp", "rep"), "tm", None, None, None),
        P(),
        P(),
        P(("dp", "rep"), None, "tm", None, None),
    )
    out_specs = (P(("dp", "rep"), "tm", None, None, None), P("tm", ("dp", "rep")))
    n = mesh.shape["tm"]
    R = mesh.shape["rep"]
    J = mesh.shape["dp"] * R
    return jax.shard_map(functools.partial(local, n, J, R), mesh=mesh, in_specs=in_specs,
                         out_specs=out_specs, check_vma=False)
```

```python
import functools
import math

import jax
import jax.numpy as jnp
from jax import lax
from jax.experimental import pallas as pl
from jax.experimental.pallas import tpu as pltpu
from jax.sharding import PartitionSpec as P

MESH = pl.DeviceIdType.MESH
BF16 = jnp.bfloat16
F32 = jnp.float32
LANES = (slice(0, 128), slice(128, 256))


def dot_nn(a, b):
    return lax.dot_general(a, b, (((1,), (0,)), ((), ())), preferred_element_type=F32)


def dot_nt(a, b):
    return lax.dot_general(a, b, (((1,), (1,)), ((), ())), preferred_element_type=F32)


def kernel(n, J, R, factor, x_hbm, w_hbm, u_hbm, g_hbm, out_ref, ug_ref,
           xs, gs, g2, u, w, wt, gt, rg, hg, hid, hidr, hs, hf, ph, phr, x32, p32, q32, s, pre, slope, of32,
           r1s, r1r, keep, r2s, r2r, r3s, r3r,
           in_sem, hf_sem, ph_sem, hg_sem, hid_sem, r1_sem, r2_sem, r3_send, r3_recv):
    H = n
    C = 256
    FW = 16
    HALF = 8 * H
    XP = 4 * H + 16
    QP = H + 16
    CB = 4 * C // J
    WIDE = -(-CB // 128) * 128
    RB = C // n
    me = lax.axis_index("tm")
    dp = lax.axis_index("dp")
    rep = lax.axis_index("rep")
    core = lax.rem(me, 2)
    myj = dp * R + rep
    is_first = me == 0
    is_last = me == n - 1
    after = lax.rem(me + 1, n)
    before = lax.rem(me + n - 1, n)

    def peer(k):
        i = n - k
        return lax.rem(me + jnp.where(lax.rem(i, 2) == 1, (i + 1) // 2, n - i // 2), n)

    def block(i):
        return pl.ds(pl.multiple_of(i * FW, FW), FW)

    def to_tm(src, dst, sems, target):
        return pltpu.make_async_remote_copy(
            src_ref=src, dst_ref=dst, send_sem=sems.at[0], recv_sem=sems.at[1],
            device_id=(target, dp, rep), device_id_type=MESH)

    def to_xy(src, dst, sems, j):
        return pltpu.make_async_remote_copy(
            src_ref=src, dst_ref=dst, send_sem=sems.at[0], recv_sem=sems.at[1],
            device_id=(me, j // R, lax.rem(j, R)), device_id_type=MESH)

    barrier = pltpu.get_barrier_semaphore()
    quarters = [pl.ds(i * n, n) for i in range(4)]
    parts = [(x_hbm, xs)]
    parts += [(w_hbm.at[a, b], w.at[a, b]) for a in (2, 1, 0) for b in range(3)]
    parts += [(g_hbm.at[rows], gs.at[rows]) for rows in quarters] + [(u_hbm, u)]
    loads = [pltpu.make_async_copy(src, dst, in_sem.at[i]) for i, (src, dst) in enumerate(parts)]
    for load in loads:
        load.start()

    def greet_tm(k, _):
        pl.semaphore_signal(barrier, inc=1, device_id=(peer(k), dp, rep), device_id_type=MESH)
        return 0

    def greet_xy(k, _):
        j = lax.rem(myj + k, J)
        pl.semaphore_signal(barrier, inc=1, device_id=(me, j // R, lax.rem(j, R)), device_id_type=MESH)
        return 0

    lax.fori_loop(1, n, greet_tm, 0)
    lax.fori_loop(1, J, greet_xy, 0)

    for f in range(6):
        x32[:, pl.ds(f * XP, 8), :] = jnp.zeros((2, 8, 128), F32)
        x32[:, pl.ds(f * XP + 8 + 4 * H, 8), :] = jnp.zeros((2, 8, 128), F32)
    for f in range(6):
        s[f, 0:H, :] = jnp.zeros((H, 3 * C), BF16)
        s[f, 5 * H : 6 * H, :] = jnp.zeros((H, 3 * C), BF16)

    def put_frame(f, value):
        for e in range(2):
            x32[e, pl.ds(f * XP + 8, 4 * H), :] = value[:, LANES[e]]

    def own_frame(f):
        return xs[pl.ds(f * H, H)].astype(F32).reshape(4 * H, C)

    loads[0].wait()
    hs[...] = xs[pl.ds(2 * H, 2 * H)].reshape(HALF, C)

    for f in range(4):
        put_frame(f + 2, own_frame(f))

    def shifts(f, _):
        for col in range(4):
            for b in range(3):
                for e in range(2):
                    v = x32[e, pl.ds(f * XP + 8 + (b - 1) * 4 + col, H, stride=4), :]
                    s[f, (col + 1) * H : (col + 2) * H, b * C + e * 128 : b * C + (e + 1) * 128] = v.astype(BF16)
        return 0

    lax.fori_loop(2, 6, shifts, 0)
    def pieces(src, dst, sems, target):
        def one(i, _):
            to_tm(src.at[block(i)], dst.at[block(i)], sems, target).start()
            return 0
        lax.fori_loop(0, HALF // FW, one, 0)

    def open_up():
        pl.semaphore_wait(barrier, n - 1 + J - 1)

        @pl.when(jnp.logical_not(is_last))
        def _():
            pieces(hs, hf, hf_sem, after)


    pre[...] = jnp.zeros((2, 2 * HALF, 128), F32)
    for load in loads[1:10]:
        load.wait()

    def taps(first, second, pair, weights):
        value = None
        for c in range(3):
            at = pl.ds(c * H, 4 * H)
            lhs = jnp.concatenate([s[pl.ds(first, 1), at, :], s[pl.ds(second, 1), at, :]], axis=0)
            part = dot_nn(lhs.reshape(HALF, 3 * C), weights(c))
            value = part if value is None else value + part
        rows = pl.ds(pl.multiple_of(pair * HALF, HALF), HALF)
        for e in range(2):
            pre[e, rows, :] += value[:, LANES[e]]

    def conv_fwd(pair, a):
        first = a + 2 * pair
        taps(first, first + 1, pair, lambda c: w[a, :, c].reshape(3 * C, C))

    def conv_step(k, _):
        @pl.when(k == 4)
        def _():
            open_up()

            @pl.when(jnp.logical_not(is_first))
            def _():
                to_tm(hs, hf, hf_sem, after).wait_recv()
                for f in range(2):
                    put_frame(f, hf[pl.ds(f * 4 * H, 4 * H), :].astype(F32))

            @pl.when(is_first)
            def _():
                for f in range(2):
                    put_frame(f, own_frame(0))

            lax.fori_loop(0, 2, shifts, 0)

        conv_fwd(jnp.where(k < 3, 1, 0), jnp.where(k < 3, 2 - k, 5 - k))
        return 0

    lax.fori_loop(0, 6, conv_step, 0)

    def act(group, _):
        for i in range(4):
            to = peer(group * 4 + i + 1)
            for e in range(2):
                v = pre[e, pl.ds(to, FW, stride=H), :]
                sig = 0.5 + 0.5 * jnp.tanh(0.5 * v)
                hid[block(to), LANES[e]] = (v * sig).astype(BF16)
                slope[block(to), LANES[e]] = sig * (1.0 + v * (1.0 - sig))
        for i in range(4):
            k = group * 4 + i + 1
            to = peer(k)

            @pl.when(k < n)
            def _():
                to_tm(hid.at[block(to)], hidr.at[block(me)], hid_sem, to).start()
        return 0

    lax.fori_loop(0, n // 4, act, 0)
    for load in loads[10:14]:
        load.wait()

    def flatten_g(i, _):
        rows = pl.ds(pl.multiple_of(i * 64, 64), 64)
        g2[rows, :] = gs[pl.ds(i * 16, 16)].reshape(64, 4 * C)
        return 0

    lax.fori_loop(0, n // 4, flatten_g, 0)
    loads[14].wait()
    rg[...] = dot_nt(g2[...], u[...]).astype(BF16)
    hg[block(me), :] = rg[block(me), :]

    def send_hg(k, _):
        to = peer(k)
        to_tm(rg.at[block(to)], hg.at[block(me)], hg_sem, to).start()
        return 0

    lax.fori_loop(1, n, send_hg, 0)
    hidr[block(me), :] = hid[block(me), :]

    def flip_g(i, _):
        at = pl.multiple_of(i * 128, 128)
        gt[pl.ds(at, 128), :] = g2[:, pl.ds(at, 128)].T
        return 0

    lax.fori_loop(0, 8, flip_g, 0)

    def flip_w(k, _):
        a, c = k // 3, lax.rem(k, 3)
        for b in range(3):
            wt[k, b * C : (b + 1) * C, :] = w[2 - a, 2 - b, 2 - c].T
        return 0

    lax.fori_loop(0, 9, flip_w, 0)
    p32[:, pl.ds(0, FW), :] = jnp.zeros((2, FW, 128), F32)
    p32[:, pl.ds((H + 1) * FW, FW), :] = jnp.zeros((2, FW, 128), F32)
    for tw in range(8):
        q32[pl.ds(tw * QP, 8), :] = jnp.zeros((8, C), F32)
        q32[pl.ds(tw * QP + 8 + H, 8), :] = jnp.zeros((8, C), F32)
    pre[...] = jnp.zeros((2, 2 * HALF, 128), F32)

    def all_blocks(src, dst, sems):
        most = pl.ds(0, (n - 1) * FW)
        return to_tm(src.at[most], dst.at[most], sems, after)

    done_hid = all_blocks(hid, hidr, hid_sem)
    done_hid.wait_recv()
    theirs = pl.ds(pl.multiple_of((1 - core) * 128, 128), 128)
    mine = pl.ds(pl.multiple_of(core * 128, 128), 128)
    JQ = J // 4

    def quarter(q):
        return pl.ds(pl.multiple_of(q * C, C), C)

    def rows_of(j):
        return pl.ds(pl.multiple_of(j * CB, CB), CB)

    def swap(q):
        return to_tm(r1s.at[quarter(q)], r1r.at[quarter(q)], r1_sem.at[q], me + 1 - 2 * core)

    def send_pair(i, _):
        part = pl.ds(pl.multiple_of(i * 64, 64), 64)
        to_tm(r1s.at[part], r1r.at[part], r1_sem.at[i // 4], me + 1 - 2 * core).start()
        return 0

    def spread(q, _):
        swap(q).wait()
        total = keep[quarter(q), :] + r1r[quarter(q), :].astype(F32)
        keep[quarter(q), :] = total
        r2s[quarter(q), :] = total.astype(BF16)
        for i in range(JQ):
            j = q * JQ + i

            @pl.when(j != myj)
            def _():
                to_xy(r2s.at[rows_of(j)], r2r.at[rows_of(myj)], r2_sem, j).start()
        return 0

    r1s[...] = dot_nn(gt[...], hidr[:, theirs]).astype(BF16)
    lax.fori_loop(0, 16, send_pair, 0)
    keep[...] = dot_nn(gt[...], hidr[:, mine])
    lax.fori_loop(0, 4, spread, 0)

    most_xy = pl.ds(0, (J - 1) * CB)
    done_r2 = to_xy(r2s.at[most_xy], r2r.at[most_xy], r2_sem, lax.rem(myj + 1, J))
    done_r2.wait_recv()
    r2r[rows_of(myj), :] = jnp.zeros((CB, 128), BF16)
    total = keep[rows_of(myj), :]
    for j in range(J):
        total = total + r2r[pl.ds(j * CB, CB), :].astype(F32)
    flipped = jnp.concatenate([total.T, jnp.zeros((128, WIDE - CB), F32)], axis=1) if WIDE > CB else total.T
    for m in range(n // 2):
        r3s[m] = flipped[m * RB : (m + 1) * RB, :]

    z = me // 2

    def r3_copy(m):
        return pltpu.make_async_remote_copy(
            src_ref=r3s.at[m], dst_ref=r3r.at[z], send_sem=r3_send.at[m], recv_sem=r3_recv.at[z],
            device_id=(core * (n // 2) + m, dp, rep), device_id_type=MESH)

    def send_r3(m, _):
        @pl.when(core * (n // 2) + m != me)
        def _():
            r3_copy(m).start()

        @pl.when(core * (n // 2) + m == me)
        def _():
            r3r[z] = r3s[m]
        return 0

    lax.fori_loop(0, n // 2, send_r3, 0)

    done_hg = all_blocks(rg, hg, hg_sem)
    done_hg.wait_recv()

    def pre_grad(i, _):
        rows = pl.ds(pl.multiple_of(i * 64, 64), 64)
        grad = (hg[rows, :].astype(F32) * slope[rows, :]).astype(BF16).astype(F32)
        for e in range(2):
            p32[e, pl.ds(pl.multiple_of(FW + i * 64, FW), 64), :] = grad[:, LANES[e]]
        return 0

    lax.fori_loop(0, n // 4, pre_grad, 0)

    def grad_shifts(t, _):
        for col in range(4):
            for b in range(3):
                for e in range(2):
                    v = p32[e, pl.ds(b * FW + t * 4 + col, H, stride=FW), :].astype(BF16)
                    s[t, (col + 1) * H : (col + 2) * H, b * C + e * 128 : b * C + (e + 1) * 128] = v
        return 0

    lax.fori_loop(0, 2, grad_shifts, 0)
    for t in range(2):
        ph[pl.ds(t * 4 * H, 4 * H), :] = s[t, H : 5 * H, C : 2 * C]

    @pl.when(jnp.logical_not(is_first))
    def _():
        pieces(ph, phr, ph_sem, before)

    lax.fori_loop(2, 4, grad_shifts, 0)

    @pl.when(is_first)
    def _():
        two = s[0].astype(F32) + s[1].astype(F32)
        s[6] = two.astype(BF16)
        s[7] = (two + s[2].astype(F32)).astype(BF16)

    def conv_back(pair, a):
        first = a + 2 * pair
        edge = jnp.logical_and(is_first, jnp.logical_and(pair == 0, a > 0))
        taps(jnp.where(edge, a + 5, first), first + 1, pair, lambda c: wt[a * 3 + c])

    back = to_tm(ph, phr, ph_sem, before)

    def back_step(k, _):
        @pl.when(k == 4)
        def _():
            @pl.when(jnp.logical_not(is_last))
            def _():
                back.wait_recv()
                for tw in range(8):
                    q32[pl.ds(tw * QP + 8, H), :] = phr[pl.ds(tw * H, H), :].astype(F32)

            @pl.when(is_last)
            def _():
                for tw in range(8):
                    q32[pl.ds(tw * QP + 8, H), :] = jnp.zeros((H, C), F32)

            for t in range(2):
                for col in range(4):
                    for b in range(3):
                        v = q32[pl.ds((t * 4 + col) * QP + 7 + b, H), :].astype(BF16)
                        s[4 + t, (col + 1) * H : (col + 2) * H, b * C : (b + 1) * C] = v

        conv_back(jnp.where(k < 3, 0, 1), jnp.where(k < 3, k, k - 3))
        return 0

    lax.fori_loop(0, 6, back_step, 0)

    for t in range(4):
        for col in range(4):
            for e in range(2):
                of32[e, pl.ds(t * 4 * H + col, H, stride=4), :] = pre[e, pl.ds((t * 4 + col) * H, H), :]
    for e in range(2):
        out_ref[:, LANES[e]] = of32[e].astype(BF16)

    def wait_r3(i, _):
        @pl.when(2 * i + me // (n // 2) != me)
        def _():
            pltpu.make_async_remote_copy(
                src_ref=r3s.at[i], dst_ref=r3r.at[i], send_sem=r3_send.at[i], recv_sem=r3_recv.at[i],
                device_id=(after, dp, rep), device_id_type=MESH).wait_recv()

        @pl.when(core * (n // 2) + i != me)
        def _():
            r3_copy(i).wait_send()
        return 0

    lax.fori_loop(0, n // 2, wait_r3, 0)
    result = r3r[0]
    for i in range(1, n // 2):
        result = result + r3r[i]
    ug_ref[...] = result[:, 0:CB] * factor

    done_hid.wait_send()
    done_hg.wait_send()
    done_r2.wait_send()

    @pl.when(jnp.logical_not(is_last))
    def _():
        to_tm(hs, hf, hf_sem, after).wait_send()

    @pl.when(jnp.logical_not(is_first))
    def _():
        back.wait_send()


def local(n, J, R, clip_frames, conv_weight, up_weight, cotangent):
    C = conv_weight.shape[-1]
    H = n
    pixels = 16 * H
    factor = 1.0 / math.sqrt(J * 4 * n * H * 4)
    x = clip_frames.reshape(4 * H, 4, C)
    g = cotangent.reshape(4 * n, 4, 4 * C)
    vmem = pl.BlockSpec(memory_space=pltpu.VMEM)
    hbm = pl.BlockSpec(memory_space=pl.ANY)
    pair = pltpu.SemaphoreType.DMA((2,))
    out, up = pl.pallas_call(
        functools.partial(kernel, n, J, R, factor),
        out_shape=(
            jax.ShapeDtypeStruct((pixels, C), BF16),
            jax.ShapeDtypeStruct((C // n, 4 * C // J), F32),
        ),
        in_specs=[hbm, hbm, hbm, hbm],
        out_specs=(vmem, vmem),
        scratch_shapes=[
            pltpu.VMEM((4 * H, 4, C), BF16),
            pltpu.VMEM((4 * n, 4, 4 * C), BF16),
            pltpu.VMEM((16 * n, 4 * C), BF16),
            pltpu.VMEM((C, 4 * C), BF16),
            pltpu.VMEM((3, 3, 3, C, C), BF16),
            pltpu.VMEM((9, 3 * C, C), BF16),
            pltpu.VMEM((4 * C, 16 * n), BF16),
            pltpu.VMEM((16 * n, C), BF16),
            pltpu.VMEM((16 * n, C), BF16),
            pltpu.VMEM((16 * n, C), BF16),
            pltpu.VMEM((16 * n, C), BF16),
            pltpu.VMEM((8 * H, C), BF16),
            pltpu.VMEM((8 * H, C), BF16),
            pltpu.VMEM((8 * H, C), BF16),
            pltpu.VMEM((8 * H, C), BF16),
            pltpu.VMEM((2, 6 * (4 * H + 16), 128), F32),
            pltpu.VMEM((2, (H + 2) * 16, 128), F32),
            pltpu.VMEM((8 * (H + 16), C), F32),
            pltpu.VMEM((8, 6 * H, 3 * C), BF16),
            pltpu.VMEM((2, pixels, 128), F32),
            pltpu.VMEM((pixels, C), F32),
            pltpu.VMEM((2, pixels, 128), F32),
            pltpu.VMEM((4 * C, C // 2), BF16),
            pltpu.VMEM((4 * C, C // 2), BF16),
            pltpu.VMEM((4 * C, C // 2), F32),
            pltpu.VMEM((4 * C, C // 2), BF16),
            pltpu.VMEM((4 * C, C // 2), BF16),
            pltpu.VMEM((n // 2, C // n, max(128, 4 * C // J)), F32),
            pltpu.VMEM((n // 2, C // n, max(128, 4 * C // J)), F32),
            pltpu.SemaphoreType.DMA((15,)),
            pair, pair, pair, pair,
            pltpu.SemaphoreType.DMA((4, 2)),
            pair,
            pltpu.SemaphoreType.DMA((n // 2,)),
            pltpu.SemaphoreType.DMA((n // 2,)),
        ],
        compiler_params=pltpu.CompilerParams(
            collective_id=0, has_side_effects=True, vmem_limit_bytes=56098816),
        cost_estimate=pl.CostEstimate(flops=4_200_000_000, bytes_accessed=6_000_000, transcendentals=131072),
    )(x, conv_weight, up_weight, g)
    return out.reshape(clip_frames.shape), up


def solution(mesh):
    in_specs = (
        P(("dp", "rep"), "tm", None, None, None),
        P(),
        P(),
        P(("dp", "rep"), None, "tm", None, None),
    )
    out_specs = (P(("dp", "rep"), "tm", None, None, None), P("tm", ("dp", "rep")))
    n = mesh.shape["tm"]
    R = mesh.shape["rep"]
    J = mesh.shape["dp"] * R
    return jax.shard_map(functools.partial(local, n, J, R), mesh=mesh, in_specs=in_specs,
                         out_specs=out_specs, check_vma=False)
```

```python
import functools
import math

import jax
import jax.numpy as jnp
from jax import lax
from jax.experimental import pallas as pl
from jax.experimental.pallas import tpu as pltpu
from jax.sharding import PartitionSpec as P

MESH = pl.DeviceIdType.MESH
BF16 = jnp.bfloat16
F32 = jnp.float32
LANES = (slice(0, 128), slice(128, 256))
SOON = 10


def dot_nn(a, b):
    return lax.dot_general(a, b, (((1,), (0,)), ((), ())), preferred_element_type=F32)


def dot_nt(a, b):
    return lax.dot_general(a, b, (((1,), (1,)), ((), ())), preferred_element_type=F32)


def kernel(n, J, R, factor, x_hbm, w_hbm, u_hbm, g_hbm, out_ref, ug_ref,
           xs, gs, g2, u, w, wt, gt, rg, hg, hid, hidr, hs, hf, ph, phr, x32, p32, q32, s, pre, slope, of32,
           r1s, r1r, keep, r2s, r2r, r3s, r3r,
           in_sem, hf_sem, ph_sem, hg_sem, hid_sem, r1_sem, r2_sem, r3_send, r3_recv):
    H = n
    C = 256
    FW = 16
    HALF = 8 * H
    XP = 4 * H + 16
    QP = H + 16
    CB = 4 * C // J
    RB = C // n
    FOLD = max(1, 128 // CB)
    RF = RB // FOLD
    me = lax.axis_index("tm")
    dp = lax.axis_index("dp")
    rep = lax.axis_index("rep")
    core = lax.rem(me, 2)
    myj = dp * R + rep
    is_first = me == 0
    is_last = me == n - 1
    after = lax.rem(me + 1, n)
    before = lax.rem(me + n - 1, n)

    def peer(k):
        i = n - k
        return lax.rem(me + jnp.where(lax.rem(i, 2) == 1, (i + 1) // 2, n - i // 2), n)

    def block(i):
        return pl.ds(pl.multiple_of(i * FW, FW), FW)

    def to_tm(src, dst, sems, target):
        return pltpu.make_async_remote_copy(
            src_ref=src, dst_ref=dst, send_sem=sems.at[0], recv_sem=sems.at[1],
            device_id=(target, dp, rep), device_id_type=MESH)

    def to_xy(src, dst, sems, j):
        return pltpu.make_async_remote_copy(
            src_ref=src, dst_ref=dst, send_sem=sems.at[0], recv_sem=sems.at[1],
            device_id=(me, j // R, lax.rem(j, R)), device_id_type=MESH)

    barrier = pltpu.get_barrier_semaphore()
    quarters = [pl.ds(i * n, n) for i in range(4)]
    parts = [(x_hbm, xs)]
    parts += [(w_hbm.at[a, b], w.at[a, b]) for a in (2, 1, 0) for b in range(3)]
    parts += [(g_hbm.at[rows], gs.at[rows]) for rows in quarters] + [(u_hbm, u)]
    loads = [pltpu.make_async_copy(src, dst, in_sem.at[i]) for i, (src, dst) in enumerate(parts)]
    for load in loads:
        load.start()

    def greet_tm(k, _):
        pl.semaphore_signal(barrier, inc=1, device_id=(peer(k), dp, rep), device_id_type=MESH)
        return 0

    def greet_xy(k, _):
        j = lax.rem(myj + k, J)
        pl.semaphore_signal(barrier, inc=1, device_id=(me, j // R, lax.rem(j, R)), device_id_type=MESH)
        return 0

    lax.fori_loop(1, n, greet_tm, 0)
    lax.fori_loop(1, J, greet_xy, 0)

    for f in range(6):
        x32[:, pl.ds(f * XP, 8), :] = jnp.zeros((2, 8, 128), F32)
        x32[:, pl.ds(f * XP + 8 + 4 * H, 8), :] = jnp.zeros((2, 8, 128), F32)
    for f in range(6):
        s[f, 0:H, :] = jnp.zeros((H, 3 * C), BF16)
        s[f, 5 * H : 6 * H, :] = jnp.zeros((H, 3 * C), BF16)

    def put_frame(f, value):
        for e in range(2):
            x32[e, pl.ds(f * XP + 8, 4 * H), :] = value[:, LANES[e]]

    def own_frame(f):
        return xs[pl.ds(f * H, H)].astype(F32).reshape(4 * H, C)

    loads[0].wait()
    hs[...] = xs[pl.ds(2 * H, 2 * H)].reshape(HALF, C)

    for f in range(4):
        put_frame(f + 2, own_frame(f))

    def shifts(f, _):
        for col in range(4):
            for b in range(3):
                for e in range(2):
                    v = x32[e, pl.ds(f * XP + 8 + (b - 1) * 4 + col, H, stride=4), :]
                    s[f, (col + 1) * H : (col + 2) * H, b * C + e * 128 : b * C + (e + 1) * 128] = v.astype(BF16)
        return 0

    lax.fori_loop(2, 6, shifts, 0)
    def pieces(src, dst, sems, target):
        def one(i, _):
            to_tm(src.at[block(i)], dst.at[block(i)], sems, target).start()
            return 0
        lax.fori_loop(0, HALF // FW, one, 0)

    def open_up():
        pl.semaphore_wait(barrier, n - 1 + J - 1)

        @pl.when(jnp.logical_not(is_last))
        def _():
            pieces(hs, hf, hf_sem, after)


    pre[...] = jnp.zeros((2, 2 * HALF, 128), F32)
    for load in loads[1:10]:
        load.wait()

    def taps(first, second, pair, weights):
        value = None
        for c in range(3):
            at = pl.ds(c * H, 4 * H)
            lhs = jnp.concatenate([s[pl.ds(first, 1), at, :], s[pl.ds(second, 1), at, :]], axis=0)
            part = dot_nn(lhs.reshape(HALF, 3 * C), weights(c))
            value = part if value is None else value + part
        rows = pl.ds(pl.multiple_of(pair * HALF, HALF), HALF)
        for e in range(2):
            pre[e, rows, :] += value[:, LANES[e]]

    def conv_fwd(pair, a):
        first = a + 2 * pair
        taps(first, first + 1, pair, lambda c: w[a, :, c].reshape(3 * C, C))

    def conv_step(k, _):
        @pl.when(k == 4)
        def _():
            open_up()

            @pl.when(jnp.logical_not(is_first))
            def _():
                to_tm(hs, hf, hf_sem, after).wait_recv()
                for f in range(2):
                    put_frame(f, hf[pl.ds(f * 4 * H, 4 * H), :].astype(F32))

            @pl.when(is_first)
            def _():
                for f in range(2):
                    put_frame(f, own_frame(0))

            lax.fori_loop(0, 2, shifts, 0)

        conv_fwd(jnp.where(k < 3, 1, 0), jnp.where(k < 3, 2 - k, 5 - k))
        return 0

    lax.fori_loop(0, 6, conv_step, 0)

    def act(group, _):
        for i in range(4):
            to = peer(group * 4 + i + 1)
            for e in range(2):
                v = pre[e, pl.ds(to, FW, stride=H), :]
                sig = 0.5 + 0.5 * jnp.tanh(0.5 * v)
                hid[block(to), LANES[e]] = (v * sig).astype(BF16)
                slope[block(to), LANES[e]] = sig * (1.0 + v * (1.0 - sig))
        for i in range(4):
            k = group * 4 + i + 1
            to = peer(k)

            @pl.when(k < n)
            def _():
                to_tm(hid.at[block(to)], hidr.at[block(me)], hid_sem, to).start()
        return 0

    lax.fori_loop(0, n // 4, act, 0)
    for load in loads[10:14]:
        load.wait()

    def flatten_g(i, _):
        rows = pl.ds(pl.multiple_of(i * 64, 64), 64)
        g2[rows, :] = gs[pl.ds(i * 16, 16)].reshape(64, 4 * C)
        return 0

    lax.fori_loop(0, n // 4, flatten_g, 0)
    loads[14].wait()
    rg[...] = dot_nt(g2[...], u[...]).astype(BF16)
    hg[block(me), :] = rg[block(me), :]

    def send_hg(k, _):
        to = peer(k)
        to_tm(rg.at[block(to)], hg.at[block(me)], hg_sem, to).start()
        return 0

    soon = min(SOON + 1, n)
    lax.fori_loop(1, soon, send_hg, 0)
    hidr[block(me), :] = hid[block(me), :]

    def flip_g(i, _):
        at = pl.multiple_of(i * 128, 128)
        gt[pl.ds(at, 128), :] = g2[:, pl.ds(at, 128)].T
        return 0

    lax.fori_loop(0, 8, flip_g, 0)

    def flip_w(k, _):
        a, c = k // 3, lax.rem(k, 3)
        for b in range(3):
            wt[k, b * C : (b + 1) * C, :] = w[2 - a, 2 - b, 2 - c].T
        return 0

    lax.fori_loop(0, 9, flip_w, 0)
    p32[:, pl.ds(0, FW), :] = jnp.zeros((2, FW, 128), F32)
    p32[:, pl.ds((H + 1) * FW, FW), :] = jnp.zeros((2, FW, 128), F32)
    for tw in range(8):
        q32[pl.ds(tw * QP, 8), :] = jnp.zeros((8, C), F32)
        q32[pl.ds(tw * QP + 8 + H, 8), :] = jnp.zeros((8, C), F32)
    pre[...] = jnp.zeros((2, 2 * HALF, 128), F32)

    def all_blocks(src, dst, sems):
        most = pl.ds(0, (n - 1) * FW)
        return to_tm(src.at[most], dst.at[most], sems, after)

    done_hid = all_blocks(hid, hidr, hid_sem)
    done_hid.wait_recv()
    lax.fori_loop(soon, n, send_hg, 0)
    theirs = pl.ds(pl.multiple_of((1 - core) * 128, 128), 128)
    mine = pl.ds(pl.multiple_of(core * 128, 128), 128)
    JQ = J // 4

    def quarter(q):
        return pl.ds(pl.multiple_of(q * C, C), C)

    def rows_of(j):
        return pl.ds(pl.multiple_of(j * CB, CB), CB)

    def swap(q):
        return to_tm(r1s.at[quarter(q)], r1r.at[quarter(q)], r1_sem.at[q], me + 1 - 2 * core)

    def send_pair(i, _):
        part = pl.ds(pl.multiple_of(i * 64, 64), 64)
        to_tm(r1s.at[part], r1r.at[part], r1_sem.at[i // 4], me + 1 - 2 * core).start()
        return 0

    def spread(q, _):
        swap(q).wait()
        total = keep[quarter(q), :] + r1r[quarter(q), :].astype(F32)
        keep[quarter(q), :] = total
        r2s[quarter(q), :] = total.astype(BF16)
        for i in range(JQ):
            j = q * JQ + i

            @pl.when(j != myj)
            def _():
                to_xy(r2s.at[rows_of(j)], r2r.at[rows_of(myj)], r2_sem, j).start()
        return 0

    r1s[...] = dot_nn(gt[...], hidr[:, theirs]).astype(BF16)
    lax.fori_loop(0, 16, send_pair, 0)
    keep[...] = dot_nn(gt[...], hidr[:, mine])
    lax.fori_loop(0, 4, spread, 0)

    most_xy = pl.ds(0, (J - 1) * CB)
    done_r2 = to_xy(r2s.at[most_xy], r2r.at[most_xy], r2_sem, lax.rem(myj + 1, J))
    done_r2.wait_recv()
    r2r[rows_of(myj), :] = jnp.zeros((CB, 128), BF16)
    total = keep[rows_of(myj), :]
    for j in range(J):
        total = total + r2r[pl.ds(j * CB, CB), :].astype(F32)
    flipped = total.T
    for m in range(n // 2):
        for i in range(FOLD):
            r3s[m, :, i * CB : (i + 1) * CB] = flipped[m * RB + i * RF : m * RB + (i + 1) * RF, :]

    z = me // 2

    def r3_copy(m):
        return pltpu.make_async_remote_copy(
            src_ref=r3s.at[m], dst_ref=r3r.at[z], send_sem=r3_send.at[m], recv_sem=r3_recv.at[z],
            device_id=(core * (n // 2) + m, dp, rep), device_id_type=MESH)

    def send_r3(m, _):
        @pl.when(core * (n // 2) + m != me)
        def _():
            r3_copy(m).start()

        @pl.when(core * (n // 2) + m == me)
        def _():
            r3r[z] = r3s[m]
        return 0

    lax.fori_loop(0, n // 2, send_r3, 0)

    done_hg = all_blocks(rg, hg, hg_sem)
    done_hg.wait_recv()

    def pre_grad(i, _):
        rows = pl.ds(pl.multiple_of(i * 64, 64), 64)
        grad = (hg[rows, :].astype(F32) * slope[rows, :]).astype(BF16).astype(F32)
        for e in range(2):
            p32[e, pl.ds(pl.multiple_of(FW + i * 64, FW), 64), :] = grad[:, LANES[e]]
        return 0

    lax.fori_loop(0, n // 4, pre_grad, 0)

    def grad_shifts(t, _):
        for col in range(4):
            for b in range(3):
                for e in range(2):
                    v = p32[e, pl.ds(b * FW + t * 4 + col, H, stride=FW), :].astype(BF16)
                    s[t, (col + 1) * H : (col + 2) * H, b * C + e * 128 : b * C + (e + 1) * 128] = v
        return 0

    lax.fori_loop(0, 2, grad_shifts, 0)
    for t in range(2):
        ph[pl.ds(t * 4 * H, 4 * H), :] = s[t, H : 5 * H, C : 2 * C]

    @pl.when(jnp.logical_not(is_first))
    def _():
        pieces(ph, phr, ph_sem, before)

    lax.fori_loop(2, 4, grad_shifts, 0)

    @pl.when(is_first)
    def _():
        two = s[0].astype(F32) + s[1].astype(F32)
        s[6] = two.astype(BF16)
        s[7] = (two + s[2].astype(F32)).astype(BF16)

    def conv_back(pair, a):
        first = a + 2 * pair
        edge = jnp.logical_and(is_first, jnp.logical_and(pair == 0, a > 0))
        taps(jnp.where(edge, a + 5, first), first + 1, pair, lambda c: wt[a * 3 + c])

    back = to_tm(ph, phr, ph_sem, before)

    def back_step(k, _):
        @pl.when(k == 4)
        def _():
            @pl.when(jnp.logical_not(is_last))
            def _():
                back.wait_recv()
                for tw in range(8):
                    q32[pl.ds(tw * QP + 8, H), :] = phr[pl.ds(tw * H, H), :].astype(F32)

            @pl.when(is_last)
            def _():
                for tw in range(8):
                    q32[pl.ds(tw * QP + 8, H), :] = jnp.zeros((H, C), F32)

            for t in range(2):
                for col in range(4):
                    for b in range(3):
                        v = q32[pl.ds((t * 4 + col) * QP + 7 + b, H), :].astype(BF16)
                        s[4 + t, (col + 1) * H : (col + 2) * H, b * C : (b + 1) * C] = v

        conv_back(jnp.where(k < 3, 0, 1), jnp.where(k < 3, k, k - 3))
        return 0

    lax.fori_loop(0, 6, back_step, 0)

    for t in range(4):
        for col in range(4):
            for e in range(2):
                of32[e, pl.ds(t * 4 * H + col, H, stride=4), :] = pre[e, pl.ds((t * 4 + col) * H, H), :]
    for e in range(2):
        out_ref[:, LANES[e]] = of32[e].astype(BF16)

    def wait_r3(i, _):
        @pl.when(2 * i + me // (n // 2) != me)
        def _():
            pltpu.make_async_remote_copy(
                src_ref=r3s.at[i], dst_ref=r3r.at[i], send_sem=r3_send.at[i], recv_sem=r3_recv.at[i],
                device_id=(after, dp, rep), device_id_type=MESH).wait_recv()

        @pl.when(core * (n // 2) + i != me)
        def _():
            r3_copy(i).wait_send()
        return 0

    lax.fori_loop(0, n // 2, wait_r3, 0)
    result = r3r[0]
    for i in range(1, n // 2):
        result = result + r3r[i]
    for i in range(FOLD):
        ug_ref[i * RF : (i + 1) * RF, :] = result[:, i * CB : (i + 1) * CB] * factor

    done_hid.wait_send()
    done_hg.wait_send()
    done_r2.wait_send()

    @pl.when(jnp.logical_not(is_last))
    def _():
        to_tm(hs, hf, hf_sem, after).wait_send()

    @pl.when(jnp.logical_not(is_first))
    def _():
        back.wait_send()


def local(n, J, R, clip_frames, conv_weight, up_weight, cotangent):
    C = conv_weight.shape[-1]
    H = n
    pixels = 16 * H
    fold = max(1, 128 * J // (4 * C))
    factor = 1.0 / math.sqrt(J * 4 * n * H * 4)
    x = clip_frames.reshape(4 * H, 4, C)
    g = cotangent.reshape(4 * n, 4, 4 * C)
    vmem = pl.BlockSpec(memory_space=pltpu.VMEM)
    hbm = pl.BlockSpec(memory_space=pl.ANY)
    pair = pltpu.SemaphoreType.DMA((2,))
    out, up = pl.pallas_call(
        functools.partial(kernel, n, J, R, factor),
        out_shape=(
            jax.ShapeDtypeStruct((pixels, C), BF16),
            jax.ShapeDtypeStruct((C // n, 4 * C // J), F32),
        ),
        in_specs=[hbm, hbm, hbm, hbm],
        out_specs=(vmem, vmem),
        scratch_shapes=[
            pltpu.VMEM((4 * H, 4, C), BF16),
            pltpu.VMEM((4 * n, 4, 4 * C), BF16),
            pltpu.VMEM((16 * n, 4 * C), BF16),
            pltpu.VMEM((C, 4 * C), BF16),
            pltpu.VMEM((3, 3, 3, C, C), BF16),
            pltpu.VMEM((9, 3 * C, C), BF16),
            pltpu.VMEM((4 * C, 16 * n), BF16),
            pltpu.VMEM((16 * n, C), BF16),
            pltpu.VMEM((16 * n, C), BF16),
            pltpu.VMEM((16 * n, C), BF16),
            pltpu.VMEM((16 * n, C), BF16),
            pltpu.VMEM((8 * H, C), BF16),
            pltpu.VMEM((8 * H, C), BF16),
            pltpu.VMEM((8 * H, C), BF16),
            pltpu.VMEM((8 * H, C), BF16),
            pltpu.VMEM((2, 6 * (4 * H + 16), 128), F32),
            pltpu.VMEM((2, (H + 2) * 16, 128), F32),
            pltpu.VMEM((8 * (H + 16), C), F32),
            pltpu.VMEM((8, 6 * H, 3 * C), BF16),
            pltpu.VMEM((2, pixels, 128), F32),
            pltpu.VMEM((pixels, C), F32),
            pltpu.VMEM((2, pixels, 128), F32),
            pltpu.VMEM((4 * C, C // 2), BF16),
            pltpu.VMEM((4 * C, C // 2), BF16),
            pltpu.VMEM((4 * C, C // 2), F32),
            pltpu.VMEM((4 * C, C // 2), BF16),
            pltpu.VMEM((4 * C, C // 2), BF16),
            pltpu.VMEM((n // 2, C // n // fold, fold * 4 * C // J), F32),
            pltpu.VMEM((n // 2, C // n // fold, fold * 4 * C // J), F32),
            pltpu.SemaphoreType.DMA((15,)),
            pair, pair, pair, pair,
            pltpu.SemaphoreType.DMA((4, 2)),
            pair,
            pltpu.SemaphoreType.DMA((n // 2,)),
            pltpu.SemaphoreType.DMA((n // 2,)),
        ],
        compiler_params=pltpu.CompilerParams(
            collective_id=0, has_side_effects=True, vmem_limit_bytes=56098816),
        cost_estimate=pl.CostEstimate(flops=4_200_000_000, bytes_accessed=6_000_000, transcendentals=131072),
    )(x, conv_weight, up_weight, g)
    return out.reshape(clip_frames.shape), up


def solution(mesh):
    in_specs = (
        P(("dp", "rep"), "tm", None, None, None),
        P(),
        P(),
        P(("dp", "rep"), None, "tm", None, None),
    )
    out_specs = (P(("dp", "rep"), "tm", None, None, None), P("tm", ("dp", "rep")))
    n = mesh.shape["tm"]
    R = mesh.shape["rep"]
    J = mesh.shape["dp"] * R
    return jax.shard_map(functools.partial(local, n, J, R), mesh=mesh, in_specs=in_specs,
                         out_specs=out_specs, check_vma=False)
```

```python
import functools
import math

import jax
import jax.numpy as jnp
from jax import lax
from jax.experimental import pallas as pl
from jax.experimental.pallas import tpu as pltpu
from jax.sharding import PartitionSpec as P

MESH = pl.DeviceIdType.MESH
BF16 = jnp.bfloat16
F32 = jnp.float32
LANES = (slice(0, 128), slice(128, 256))
SOON = 10


def dot_nn(a, b):
    return lax.dot_general(a, b, (((1,), (0,)), ((), ())), preferred_element_type=F32)


def dot_nt(a, b):
    return lax.dot_general(a, b, (((1,), (1,)), ((), ())), preferred_element_type=F32)


def kernel(n, J, R, factor, x_hbm, w_hbm, u_hbm, g_hbm, out_ref, ug_ref,
           xs, gs, g2, u, w, wt, gt, rg, hg, hid, hidr, hs, hf, ph, phr, x32, p32, q32, s, pre, slope, of32,
           r1s, r1r, keep, r2s, r2r, r3s, r3r,
           in_sem, hf_sem, ph_sem, hg_sem, hid_sem, r1_sem, r2_sem, r3_send, r3_recv):
    H = n
    C = 256
    FW = 16
    HALF = 8 * H
    XP = 4 * H + 16
    QP = H + 16
    CB = 4 * C // J
    RB = C // n
    FOLD = max(1, 128 // CB)
    RF = RB // FOLD
    me = lax.axis_index("tm")
    dp = lax.axis_index("dp")
    rep = lax.axis_index("rep")
    core = lax.rem(me, 2)
    myj = dp * R + rep
    is_first = me == 0
    is_last = me == n - 1
    after = lax.rem(me + 1, n)
    before = lax.rem(me + n - 1, n)

    def peer(k):
        i = n - k
        return lax.rem(me + jnp.where(lax.rem(i, 2) == 1, (i + 1) // 2, n - i // 2), n)

    def block(i):
        return pl.ds(pl.multiple_of(i * FW, FW), FW)

    def to_tm(src, dst, sems, target):
        return pltpu.make_async_remote_copy(
            src_ref=src, dst_ref=dst, send_sem=sems.at[0], recv_sem=sems.at[1],
            device_id=(target, dp, rep), device_id_type=MESH)

    def to_xy(src, dst, sems, j):
        return pltpu.make_async_remote_copy(
            src_ref=src, dst_ref=dst, send_sem=sems.at[0], recv_sem=sems.at[1],
            device_id=(me, j // R, lax.rem(j, R)), device_id_type=MESH)

    barrier = pltpu.get_barrier_semaphore()
    quarters = [pl.ds(i * n, n) for i in range(4)]
    parts = [(x_hbm, xs)]
    parts += [(w_hbm.at[a, b], w.at[a, b]) for a in (2, 1, 0) for b in range(3)]
    parts += [(g_hbm.at[rows], gs.at[rows]) for rows in quarters] + [(u_hbm, u)]
    loads = [pltpu.make_async_copy(src, dst, in_sem.at[i]) for i, (src, dst) in enumerate(parts)]
    for load in loads:
        load.start()

    def greet_tm(k, _):
        pl.semaphore_signal(barrier, inc=1, device_id=(peer(k), dp, rep), device_id_type=MESH)
        return 0

    def greet_xy(k, _):
        j = lax.rem(myj + k, J)
        pl.semaphore_signal(barrier, inc=1, device_id=(me, j // R, lax.rem(j, R)), device_id_type=MESH)
        return 0

    lax.fori_loop(1, n, greet_tm, 0)
    lax.fori_loop(1, J, greet_xy, 0)

    for f in range(6):
        x32[:, pl.ds(f * XP, 8), :] = jnp.zeros((2, 8, 128), F32)
        x32[:, pl.ds(f * XP + 8 + 4 * H, 8), :] = jnp.zeros((2, 8, 128), F32)
    for f in range(6):
        s[f, 0:H, :] = jnp.zeros((H, 3 * C), BF16)
        s[f, 5 * H : 6 * H, :] = jnp.zeros((H, 3 * C), BF16)

    def put_frame(f, value):
        for e in range(2):
            x32[e, pl.ds(f * XP + 8, 4 * H), :] = value[:, LANES[e]]

    def own_frame(f):
        return xs[pl.ds(f * H, H)].astype(F32).reshape(4 * H, C)

    loads[0].wait()
    hs[...] = xs[pl.ds(2 * H, 2 * H)].reshape(HALF, C)

    for f in range(4):
        put_frame(f + 2, own_frame(f))

    def shifts(f, _):
        for col in range(4):
            for b in range(3):
                for e in range(2):
                    v = x32[e, pl.ds(f * XP + 8 + (b - 1) * 4 + col, H, stride=4), :]
                    s[f, (col + 1) * H : (col + 2) * H, b * C + e * 128 : b * C + (e + 1) * 128] = v.astype(BF16)
        return 0

    lax.fori_loop(2, 6, shifts, 0)
    def pieces(src, dst, sems, target):
        def one(i, _):
            to_tm(src.at[block(i)], dst.at[block(i)], sems, target).start()
            return 0
        lax.fori_loop(0, HALF // FW, one, 0)

    def open_up():
        pl.semaphore_wait(barrier, n - 1 + J - 1)

        @pl.when(jnp.logical_not(is_last))
        def _():
            pieces(hs, hf, hf_sem, after)


    pre[...] = jnp.zeros((2, 2 * HALF, 128), F32)
    for load in loads[1:10]:
        load.wait()

    def taps(first, second, pair, weights):
        value = None
        for c in range(3):
            at = pl.ds(c * H, 4 * H)
            lhs = jnp.concatenate([s[pl.ds(first, 1), at, :], s[pl.ds(second, 1), at, :]], axis=0)
            part = dot_nn(lhs.reshape(HALF, 3 * C), weights(c))
            value = part if value is None else value + part
        rows = pl.ds(pl.multiple_of(pair * HALF, HALF), HALF)
        for e in range(2):
            pre[e, rows, :] += value[:, LANES[e]]

    def conv_fwd(pair, a):
        first = a + 2 * pair
        taps(first, first + 1, pair, lambda c: w[a, :, c].reshape(3 * C, C))

    def conv_step(k, _):
        @pl.when(k == 4)
        def _():
            open_up()

            @pl.when(jnp.logical_not(is_first))
            def _():
                to_tm(hs, hf, hf_sem, after).wait_recv()
                for f in range(2):
                    put_frame(f, hf[pl.ds(f * 4 * H, 4 * H), :].astype(F32))

            @pl.when(is_first)
            def _():
                for f in range(2):
                    put_frame(f, own_frame(0))

            lax.fori_loop(0, 2, shifts, 0)

        conv_fwd(jnp.where(k < 3, 1, 0), jnp.where(k < 3, 2 - k, 5 - k))
        return 0

    lax.fori_loop(0, 6, conv_step, 0)

    def act(group, _):
        for i in range(4):
            to = peer(group * 4 + i + 1)
            for e in range(2):
                v = pre[e, pl.ds(to, FW, stride=H), :]
                sig = 0.5 + 0.5 * jnp.tanh(0.5 * v)
                hid[block(to), LANES[e]] = (v * sig).astype(BF16)
        for i in range(4):
            k = group * 4 + i + 1
            to = peer(k)

            @pl.when(k < n)
            def _():
                to_tm(hid.at[block(to)], hidr.at[block(me)], hid_sem, to).start()
        return 0

    lax.fori_loop(0, n // 4, act, 0)
    for load in loads[10:14]:
        load.wait()

    def flatten_g(i, _):
        rows = pl.ds(pl.multiple_of(i * 64, 64), 64)
        g2[rows, :] = gs[pl.ds(i * 16, 16)].reshape(64, 4 * C)
        return 0

    lax.fori_loop(0, n // 4, flatten_g, 0)
    loads[14].wait()
    rg[...] = dot_nt(g2[...], u[...]).astype(BF16)
    hg[block(me), :] = rg[block(me), :]

    def send_hg(k, _):
        to = peer(k)
        to_tm(rg.at[block(to)], hg.at[block(me)], hg_sem, to).start()
        return 0

    soon = min(SOON + 1, n)
    lax.fori_loop(1, soon, send_hg, 0)
    hidr[block(me), :] = hid[block(me), :]

    def flip_g(i, _):
        at = pl.multiple_of(i * 128, 128)
        gt[pl.ds(at, 128), :] = g2[:, pl.ds(at, 128)].T
        return 0

    lax.fori_loop(0, 8, flip_g, 0)

    def flip_w(k, _):
        a, c = k // 3, lax.rem(k, 3)
        for b in range(3):
            wt[k, b * C : (b + 1) * C, :] = w[2 - a, 2 - b, 2 - c].T
        return 0

    lax.fori_loop(0, 9, flip_w, 0)

    def slopes(group, _):
        for i in range(4):
            row = group * 4 + i
            for e in range(2):
                v = pre[e, pl.ds(row, FW, stride=H), :]
                sig = 0.5 + 0.5 * jnp.tanh(0.5 * v)
                slope[block(row), LANES[e]] = sig * (1.0 + v * (1.0 - sig))
        return 0

    lax.fori_loop(0, n // 4, slopes, 0)
    p32[:, pl.ds(0, FW), :] = jnp.zeros((2, FW, 128), F32)
    p32[:, pl.ds((H + 1) * FW, FW), :] = jnp.zeros((2, FW, 128), F32)
    for tw in range(8):
        q32[pl.ds(tw * QP, 8), :] = jnp.zeros((8, C), F32)
        q32[pl.ds(tw * QP + 8 + H, 8), :] = jnp.zeros((8, C), F32)
    pre[...] = jnp.zeros((2, 2 * HALF, 128), F32)

    def all_blocks(src, dst, sems):
        most = pl.ds(0, (n - 1) * FW)
        return to_tm(src.at[most], dst.at[most], sems, after)

    done_hid = all_blocks(hid, hidr, hid_sem)
    done_hid.wait_recv()
    theirs = pl.ds(pl.multiple_of((1 - core) * 128, 128), 128)
    mine = pl.ds(pl.multiple_of(core * 128, 128), 128)
    JQ = J // 4

    def quarter(q):
        return pl.ds(pl.multiple_of(q * C, C), C)

    def rows_of(j):
        return pl.ds(pl.multiple_of(j * CB, CB), CB)

    def swap(q):
        return to_tm(r1s.at[quarter(q)], r1r.at[quarter(q)], r1_sem.at[q], me + 1 - 2 * core)

    def send_pair(i, _):
        part = pl.ds(pl.multiple_of(i * 64, 64), 64)
        to_tm(r1s.at[part], r1r.at[part], r1_sem.at[i // 4], me + 1 - 2 * core).start()
        return 0

    def spread(q, _):
        swap(q).wait()
        total = keep[quarter(q), :] + r1r[quarter(q), :].astype(F32)
        keep[quarter(q), :] = total
        r2s[quarter(q), :] = total.astype(BF16)
        for i in range(JQ):
            j = q * JQ + i

            @pl.when(j != myj)
            def _():
                to_xy(r2s.at[rows_of(j)], r2r.at[rows_of(myj)], r2_sem, j).start()
        return 0

    r1s[...] = dot_nn(gt[...], hidr[:, theirs]).astype(BF16)
    lax.fori_loop(0, 16, send_pair, 0)
    lax.fori_loop(soon, n, send_hg, 0)
    keep[...] = dot_nn(gt[...], hidr[:, mine])
    lax.fori_loop(0, 4, spread, 0)

    most_xy = pl.ds(0, (J - 1) * CB)
    done_r2 = to_xy(r2s.at[most_xy], r2r.at[most_xy], r2_sem, lax.rem(myj + 1, J))
    done_r2.wait_recv()
    r2r[rows_of(myj), :] = jnp.zeros((CB, 128), BF16)
    total = keep[rows_of(myj), :]
    for j in range(J):
        total = total + r2r[pl.ds(j * CB, CB), :].astype(F32)
    flipped = total.T
    for m in range(n // 2):
        for i in range(FOLD):
            r3s[m, :, i * CB : (i + 1) * CB] = flipped[m * RB + i * RF : m * RB + (i + 1) * RF, :]

    z = me // 2

    def r3_copy(m):
        return pltpu.make_async_remote_copy(
            src_ref=r3s.at[m], dst_ref=r3r.at[z], send_sem=r3_send.at[m], recv_sem=r3_recv.at[z],
            device_id=(core * (n // 2) + m, dp, rep), device_id_type=MESH)

    def send_r3(m, _):
        @pl.when(core * (n // 2) + m != me)
        def _():
            r3_copy(m).start()

        @pl.when(core * (n // 2) + m == me)
        def _():
            r3r[z] = r3s[m]
        return 0

    lax.fori_loop(0, n // 2, send_r3, 0)

    done_hg = all_blocks(rg, hg, hg_sem)
    done_hg.wait_recv()

    def pre_grad(i, _):
        rows = pl.ds(pl.multiple_of(i * 64, 64), 64)
        grad = (hg[rows, :].astype(F32) * slope[rows, :]).astype(BF16).astype(F32)
        for e in range(2):
            p32[e, pl.ds(pl.multiple_of(FW + i * 64, FW), 64), :] = grad[:, LANES[e]]
        return 0

    lax.fori_loop(0, n // 4, pre_grad, 0)

    def grad_shifts(t, _):
        for col in range(4):
            for b in range(3):
                for e in range(2):
                    v = p32[e, pl.ds(b * FW + t * 4 + col, H, stride=FW), :].astype(BF16)
                    s[t, (col + 1) * H : (col + 2) * H, b * C + e * 128 : b * C + (e + 1) * 128] = v
        return 0

    lax.fori_loop(0, 2, grad_shifts, 0)
    for t in range(2):
        ph[pl.ds(t * 4 * H, 4 * H), :] = s[t, H : 5 * H, C : 2 * C]

    @pl.when(jnp.logical_not(is_first))
    def _():
        pieces(ph, phr, ph_sem, before)

    lax.fori_loop(2, 4, grad_shifts, 0)

    @pl.when(is_first)
    def _():
        two = s[0].astype(F32) + s[1].astype(F32)
        s[6] = two.astype(BF16)
        s[7] = (two + s[2].astype(F32)).astype(BF16)

    def conv_back(pair, a):
        first = a + 2 * pair
        edge = jnp.logical_and(is_first, jnp.logical_and(pair == 0, a > 0))
        taps(jnp.where(edge, a + 5, first), first + 1, pair, lambda c: wt[a * 3 + c])

    back = to_tm(ph, phr, ph_sem, before)

    def back_step(k, _):
        @pl.when(k == 4)
        def _():
            @pl.when(jnp.logical_not(is_last))
            def _():
                back.wait_recv()
                for tw in range(8):
                    q32[pl.ds(tw * QP + 8, H), :] = phr[pl.ds(tw * H, H), :].astype(F32)

            @pl.when(is_last)
            def _():
                for tw in range(8):
                    q32[pl.ds(tw * QP + 8, H), :] = jnp.zeros((H, C), F32)

            for t in range(2):
                for col in range(4):
                    for b in range(3):
                        v = q32[pl.ds((t * 4 + col) * QP + 7 + b, H), :].astype(BF16)
                        s[4 + t, (col + 1) * H : (col + 2) * H, b * C : (b + 1) * C] = v

        conv_back(jnp.where(k < 3, 0, 1), jnp.where(k < 3, k, k - 3))
        return 0

    lax.fori_loop(0, 6, back_step, 0)

    for t in range(4):
        for col in range(4):
            for e in range(2):
                of32[e, pl.ds(t * 4 * H + col, H, stride=4), :] = pre[e, pl.ds((t * 4 + col) * H, H), :]
    for e in range(2):
        out_ref[:, LANES[e]] = of32[e].astype(BF16)

    def wait_r3(i, _):
        @pl.when(2 * i + me // (n // 2) != me)
        def _():
            pltpu.make_async_remote_copy(
                src_ref=r3s.at[i], dst_ref=r3r.at[i], send_sem=r3_send.at[i], recv_sem=r3_recv.at[i],
                device_id=(after, dp, rep), device_id_type=MESH).wait_recv()

        @pl.when(core * (n // 2) + i != me)
        def _():
            r3_copy(i).wait_send()
        return 0

    lax.fori_loop(0, n // 2, wait_r3, 0)
    result = r3r[0]
    for i in range(1, n // 2):
        result = result + r3r[i]
    for i in range(FOLD):
        ug_ref[i * RF : (i + 1) * RF, :] = result[:, i * CB : (i + 1) * CB] * factor

    done_hid.wait_send()
    done_hg.wait_send()
    done_r2.wait_send()

    @pl.when(jnp.logical_not(is_last))
    def _():
        to_tm(hs, hf, hf_sem, after).wait_send()

    @pl.when(jnp.logical_not(is_first))
    def _():
        back.wait_send()


def local(n, J, R, clip_frames, conv_weight, up_weight, cotangent):
    C = conv_weight.shape[-1]
    H = n
    pixels = 16 * H
    fold = max(1, 128 * J // (4 * C))
    factor = 1.0 / math.sqrt(J * 4 * n * H * 4)
    x = clip_frames.reshape(4 * H, 4, C)
    g = cotangent.reshape(4 * n, 4, 4 * C)
    vmem = pl.BlockSpec(memory_space=pltpu.VMEM)
    hbm = pl.BlockSpec(memory_space=pl.ANY)
    pair = pltpu.SemaphoreType.DMA((2,))
    out, up = pl.pallas_call(
        functools.partial(kernel, n, J, R, factor),
        out_shape=(
            jax.ShapeDtypeStruct((pixels, C), BF16),
            jax.ShapeDtypeStruct((C // n, 4 * C // J), F32),
        ),
        in_specs=[hbm, hbm, hbm, hbm],
        out_specs=(vmem, vmem),
        scratch_shapes=[
            pltpu.VMEM((4 * H, 4, C), BF16),
            pltpu.VMEM((4 * n, 4, 4 * C), BF16),
            pltpu.VMEM((16 * n, 4 * C), BF16),
            pltpu.VMEM((C, 4 * C), BF16),
            pltpu.VMEM((3, 3, 3, C, C), BF16),
            pltpu.VMEM((9, 3 * C, C), BF16),
            pltpu.VMEM((4 * C, 16 * n), BF16),
            pltpu.VMEM((16 * n, C), BF16),
            pltpu.VMEM((16 * n, C), BF16),
            pltpu.VMEM((16 * n, C), BF16),
            pltpu.VMEM((16 * n, C), BF16),
            pltpu.VMEM((8 * H, C), BF16),
            pltpu.VMEM((8 * H, C), BF16),
            pltpu.VMEM((8 * H, C), BF16),
            pltpu.VMEM((8 * H, C), BF16),
            pltpu.VMEM((2, 6 * (4 * H + 16), 128), F32),
            pltpu.VMEM((2, (H + 2) * 16, 128), F32),
            pltpu.VMEM((8 * (H + 16), C), F32),
            pltpu.VMEM((8, 6 * H, 3 * C), BF16),
            pltpu.VMEM((2, pixels, 128), F32),
            pltpu.VMEM((pixels, C), F32),
            pltpu.VMEM((2, pixels, 128), F32),
            pltpu.VMEM((4 * C, C // 2), BF16),
            pltpu.VMEM((4 * C, C // 2), BF16),
            pltpu.VMEM((4 * C, C // 2), F32),
            pltpu.VMEM((4 * C, C // 2), BF16),
            pltpu.VMEM((4 * C, C // 2), BF16),
            pltpu.VMEM((n // 2, C // n // fold, fold * 4 * C // J), F32),
            pltpu.VMEM((n // 2, C // n // fold, fold * 4 * C // J), F32),
            pltpu.SemaphoreType.DMA((15,)),
            pair, pair, pair, pair,
            pltpu.SemaphoreType.DMA((4, 2)),
            pair,
            pltpu.SemaphoreType.DMA((n // 2,)),
            pltpu.SemaphoreType.DMA((n // 2,)),
        ],
        compiler_params=pltpu.CompilerParams(
            collective_id=0, has_side_effects=True, vmem_limit_bytes=56098816),
        cost_estimate=pl.CostEstimate(flops=4_200_000_000, bytes_accessed=6_000_000, transcendentals=131072),
    )(x, conv_weight, up_weight, g)
    return out.reshape(clip_frames.shape), up


def solution(mesh):
    in_specs = (
        P(("dp", "rep"), "tm", None, None, None),
        P(),
        P(),
        P(("dp", "rep"), None, "tm", None, None),
    )
    out_specs = (P(("dp", "rep"), "tm", None, None, None), P("tm", ("dp", "rep")))
    n = mesh.shape["tm"]
    R = mesh.shape["rep"]
    J = mesh.shape["dp"] * R
    return jax.shard_map(functools.partial(local, n, J, R), mesh=mesh, in_specs=in_specs,
                         out_specs=out_specs, check_vma=False)
```
